256 devices in a mesh: ctx: 64 (over y, z, x_lo), head: 4 (over x_hi, core).
Axes of the slice: x: 4 (x_hi: 2, x_lo: 2; x = x_hi * 2 + x_lo), y: 4, z: 8, core: 2. Of those that a mesh axis runs over, the one named last changes fastest.
Arguments:
- queries: bfloat16 [16384, 2048], P('ctx', 'head'), may hold values from -32 to 32
- keys: bfloat16 [16384, 1024], P('ctx', 'head'), may hold values from -32 to 32
- values: bfloat16 [16384, 1024], P('ctx', 'head'), may hold values from -6 to 6
- doc_ids: int32 [128], replicated, may hold values from 0 to 7, as said below
- out_weight: bfloat16 [2048, 5376], P('head'), may hold values from -1 to 1
Outputs:
- projected: bfloat16 [16384, 5376], P(('ctx', 'head'))
The draws below stay inside these ranges and needn't reach their ends.
Inputs may be any that keep to these rules, and one draw needn't show every extreme that they name: doc_ids is non-decreasing along the sequence and starts at 0; the first document spans exactly 96 blocks, every other one 1 or more blocks.
All inputs are finite; a program needn't handle non-finite values.
Results may differ from the reference program's by a relative error of at most 0.015.
Values may be sent and summed in bfloat16 or wider, within the bound.
A program may use at most 64 MiB of HBM per device.

```python
import math
import jax
import jax.numpy as jnp
from jax import lax

D = 5376
QUERY_HEADS = 16
KEY_VALUE_HEADS = 8
HEAD_SIZE = 128
BLOCK = 128
PACKED_TOKENS = 16384
NBLK = 128
DOCS = 8
LONGEST = 96


def draw_queries(key, part):
    key = jax.random.fold_in(key, 1)
    query_group = QUERY_HEADS // KEY_VALUE_HEADS
    main_portion = jax.random.normal(key, (PACKED_TOKENS, KEY_VALUE_HEADS, query_group, HEAD_SIZE), jnp.float32)
    return main_portion.reshape(PACKED_TOKENS, QUERY_HEADS * HEAD_SIZE).astype(jnp.bfloat16)


def draw_keys(key, part):
    key = jax.random.fold_in(key, 2)
    main_portion = jax.random.normal(key, (PACKED_TOKENS, KEY_VALUE_HEADS, HEAD_SIZE), jnp.float32)
    return main_portion.reshape(PACKED_TOKENS, KEY_VALUE_HEADS * HEAD_SIZE).astype(jnp.bfloat16)


def draw_doc_ids(key, part):
    key = jax.random.fold_in(key, 3)
    candidates = NBLK - LONGEST - 1
    order = jax.random.permutation(key, candidates).astype(jnp.int32)
    chosen = order[:DOCS - 2] + LONGEST + 1
    blocks = jnp.arange(NBLK, dtype=jnp.int32)
    after_first = (blocks >= LONGEST).astype(jnp.int32)
    past_cuts = jnp.sum((blocks[:, None] >= chosen[None, :]).astype(jnp.int32), axis=1)
    return (after_first + past_cuts).astype(jnp.int32)


def shard_levels(rng, shape, pieces, smallest, largest):
    level, own = 1.0, jax.random.fold_in(rng, 6)
    for position, blocks in pieces:
        draws = jnp.exp(jax.random.uniform(jax.random.fold_in(own, position), (blocks,), jnp.float32, smallest / len(pieces), largest / len(pieces)))
        level = level * jnp.repeat(draws, shape[position] // blocks).reshape([-1 if axis == position else 1 for axis in range(len(shape))])
    return level


def normal_values(rng, extent, deviation, reach, shards=(), kind=jnp.bfloat16):
    values = jax.random.normal(rng, extent, jnp.float32) * deviation
    if len(shards) > 0:
        values = shard_levels(rng, extent, shards, -0.22, 0.18) * values
    return jnp.clip(values, min=-reach, max=reach).astype(kind)


def setup_inputs(seed: int = 0) -> dict:
    seeds = jax.random.split(jax.random.key(seed), 6)
    queries = draw_queries(jax.random.fold_in(seeds[5], 71), 0)
    keys = draw_keys(jax.random.fold_in(seeds[5], 71), 0)
    values = normal_values(seeds[2], (PACKED_TOKENS, KEY_VALUE_HEADS * HEAD_SIZE), 1.0, 6.0, ((0, 64), (1, 4)))
    doc_ids = draw_doc_ids(jax.random.fold_in(seeds[5], 71), 0)
    out_weight = normal_values(seeds[4], (QUERY_HEADS * HEAD_SIZE, D), (QUERY_HEADS * HEAD_SIZE // 64) ** -0.5, 1.0, ((0, 4),))
    return dict(queries=queries, keys=keys, values=values, doc_ids=doc_ids, out_weight=out_weight)


def reference(queries, keys, values, doc_ids, out_weight):
    query_group = QUERY_HEADS // KEY_VALUE_HEADS
    scale = 168.0 ** -0.5
    tok_doc = jnp.repeat(doc_ids, BLOCK)
    key_pos = jnp.arange(PACKED_TOKENS, dtype=jnp.int32)
    key_head_rows = keys.reshape(PACKED_TOKENS, KEY_VALUE_HEADS, HEAD_SIZE).astype(jnp.float32)
    value_head_rows = values.reshape(PACKED_TOKENS, KEY_VALUE_HEADS, HEAD_SIZE).astype(jnp.float32)
    token_rows = math.gcd(PACKED_TOKENS, 512)

    def one_block(start):
        mask_block = lax.dynamic_slice_in_dim(queries, start, token_rows, 0)
        mask_block = mask_block.reshape(token_rows, KEY_VALUE_HEADS, query_group, HEAD_SIZE).astype(jnp.float32)
        scores = jnp.einsum("qkgd,skd->kgqs", mask_block, key_head_rows) * scale
        q_pos = start + jnp.arange(token_rows, dtype=jnp.int32)
        q_doc = lax.dynamic_slice_in_dim(tok_doc, start, token_rows, 0)
        allowed = (q_doc[:, None] == tok_doc[None, :]) & (q_pos[:, None] >= key_pos[None, :])
        scores = jnp.where(allowed, scores, -1e30)
        peak = jnp.max(scores, axis=-1, keepdims=True)
        weights = jnp.exp(scores - peak)
        totals = jnp.sum(weights, axis=-1)
        rounded = weights.astype(jnp.bfloat16).astype(jnp.float32)
        summed = jnp.einsum("kgqs,skd->qkgd", rounded, value_head_rows)
        result = summed / jnp.transpose(totals, (2, 0, 1))[..., None]
        return result.reshape(token_rows, QUERY_HEADS * HEAD_SIZE).astype(jnp.bfloat16)

    starts = jnp.arange(PACKED_TOKENS // token_rows, dtype=jnp.int32) * token_rows
    attended = lax.map(one_block, starts).reshape(PACKED_TOKENS, QUERY_HEADS * HEAD_SIZE)
    return jnp.dot(attended, out_weight, preferred_element_type=jnp.float32).astype(jnp.bfloat16)
```

```python
import functools

import jax
import jax.numpy as jnp
import numpy as np
from jax import lax
from jax.experimental import pallas as pl
from jax.experimental.pallas import tpu as pltpu
from jax.sharding import PartitionSpec as P

MESH = pl.DeviceIdType.MESH
HD = 128
T = 256
NY, NZ, NX = 4, 8, 2
D = 5376
CH = 768
NCH = D // CH
QSCALE = float(168.0 ** (-0.5) * np.log2(np.e))
NEG = -1e30


def kernel(
    q_ref, k_ref, v_ref, doc_ref, w_ref, o_ref,
    w_vm, qsrc, ksrc, kv, q_in, qt, m_s, l_s, acc, o_out, st_out, o_in, st_in,
    att, p_own, p_sib, sib_in, cut_out, cut_in,
    w_sem, a_kv_s, a_q_s, r_sem, f_sem, h_s, h_r, q_r, ot_s, ot_r, st_s, st_r,
    sb_s, sb_r, cu_s, cu_r,
):
    ctx, head = lax.axis_index("ctx"), lax.axis_index("head")
    y, z, x = ctx // 16, (ctx // 2) % 8, ctx % 2
    xh, c = head // 2, head % 2

    def dev(yy, zz, xx, cc, hh=xh):
        return {"ctx": (yy * 8 + zz) * 2 + xx, "head": hh * 2 + cc}

    def remote(src, dst, s, r, to):
        return pltpu.make_async_remote_copy(
            src_ref=src, dst_ref=dst, send_sem=s, recv_sem=r, device_id=to, device_id_type=MESH
        )

    barrier = pltpu.get_barrier_semaphore()

    def greet(to):
        pl.semaphore_signal(barrier, inc=1, device_id=to, device_id_type=MESH)

    for i in range(1, 16):
        greet(dev((y + i // 4) % 4, z, (x + (i // 2) % 2) % 2, (c + i) % 2))
    up, down = (z + 1) % 8, (z + 7) % 8
    greet(dev(y, up, x, c))
    greet(dev(y, down, x, c))
    greet(dev(y, z, x, c, 1 - xh))

    w_copy = pltpu.make_async_copy(w_ref, w_vm, w_sem)
    w_copy.start()

    for i in range(2):
        ksrc[0, i] = k_ref[:, i * HD:(i + 1) * HD]
        for t in range(2):
            part = v_ref[t * HD:(t + 1) * HD, i * HD:(i + 1) * HD]
            ksrc[1, i, t * HD:(t + 1) * HD, :] = part.astype(jnp.float32).T.astype(jnp.bfloat16)
    for j in range(4):
        part = q_ref[:, j * HD:(j + 1) * HD]
        qsrc[j] = part.astype(jnp.float32).T.astype(jnp.bfloat16)
    m_s[...] = jnp.full(m_s.shape, NEG, jnp.float32)
    l_s[...] = jnp.zeros(l_s.shape, jnp.float32)
    acc[...] = jnp.zeros(acc.shape, jnp.float32)

    pl.semaphore_wait(barrier, 18)

    def kv_copy(i, n):
        return remote(
            ksrc.at[n, i], kv.at[n, z, y], a_kv_s.at[n, i], r_sem.at[0, y], dev(2 * c + i, z, x, n)
        )

    def kv_self(i, n):
        return (2 * c + i == y) & (c == n)

    def q_copy(j, xx):
        return remote(
            qsrc.at[j], q_in.at[y, x], a_q_s.at[j, xx], q_r.at[y, x],
            dev(2 * c + j // 2, z, xx, j % 2),
        )

    def q_self(j, xx):
        return (2 * c + j // 2 == y) & (c == j % 2) & (xx == x)

    def either(cond, there, here):
        @pl.when(jnp.logical_not(cond))
        def _():
            there()

        if here is not None:

            @pl.when(cond)
            def _():
                here()

    for i in range(2):
        for n in range(2):
            either(
                kv_self(i, n),
                lambda i=i, n=n: kv_copy(i, n).start(),
                lambda i=i, n=n: pltpu.make_async_copy(
                    ksrc.at[n, i], kv.at[n, z, y], r_sem.at[0, y]
                ).start(),
            )
    for j in range(4):
        for xx in range(2):
            either(
                q_self(j, xx),
                lambda j=j, xx=xx: q_copy(j, xx).start(),
                lambda j=j, xx=xx: pltpu.make_async_copy(
                    qsrc.at[j], q_in.at[y, x], q_r.at[y, x]
                ).start(),
            )

    def place(s):
        dist = (s + 1) // 2
        return (z + 8 + jnp.where(s % 2 == 1, -dist, dist)) % 8

    def pass_on(s, yk, to_slot, to_z):
        zz = place(s)
        return remote(
            kv.at[c, zz, yk], kv.at[c, zz, yk], f_sem.at[to_slot, yk], r_sem.at[to_slot, yk],
            dev(y, to_z, x, c),
        )

    def share(s, yk):
        zz = place(s)
        return remote(
            kv.at[c, zz, yk], kv.at[c, zz, yk], h_s.at[s, yk], h_r.at[s, yk], dev(y, z, x, 1 - c)
        )

    def landed(ref, sem):
        pltpu.make_async_copy(ref, ref, sem).wait()

    def forwards(s, yk, act):
        @pl.when(s == 0)
        def _():
            act(pass_on(s, yk, 1, up))
            act(pass_on(s, yk, 2, down))

        @pl.when((s > 0) & (s < 5))
        def _():
            act(pass_on(s, yk, s + 2, jnp.where(s % 2 == 1, up, down)))

        @pl.when((s == 5) & (c == 0))
        def _():
            act(pass_on(s, yk, 7, up))

        @pl.when((s == 6) & (c == 1))
        def _():
            act(pass_on(s, yk, 7, down))

    def comm(e):
        s, yk = e // 4, (e + 3) % 4
        landed(kv.at[c, place(s), yk], r_sem.at[s, yk])
        forwards(s, yk, lambda copy: copy.start())
        share(s, yk).start()

    def attend(yq, zz, yk, masked):
        kb = kv[0, zz, yk]
        vb = kv[1, zz, yk]
        vt = jnp.concatenate([vb[:HD], vb[HD:]], axis=1)
        scores = jnp.dot(
            jnp.concatenate([kb, kb], axis=1), qt[yq], preferred_element_type=jnp.float32
        )
        if masked:
            row = lax.broadcasted_iota(jnp.int32, (T, 1), 0)
            col = lax.broadcasted_iota(jnp.int32, (1, 2 * T), 1)
            kbase, qbase = (16 * yk + 2 * zz + x) * 2, (16 * yq + 2 * z) * 2
            kdoc = jnp.where(row < HD, doc_ref[kbase], doc_ref[kbase + 1])
            qdoc = jnp.where(
                col < HD, doc_ref[qbase],
                jnp.where(
                    col < 2 * HD, doc_ref[qbase + 1],
                    jnp.where(col < 3 * HD, doc_ref[qbase + 2], doc_ref[qbase + 3]),
                ),
            )
            allowed = (kdoc == qdoc) & (row + kbase * HD <= col + qbase * HD)
            scores = jnp.where(allowed, scores, NEG)
        old = m_s[yq]
        new = jnp.maximum(old, jnp.max(scores, axis=0, keepdims=True))
        weights = jnp.exp2(scores - new)
        shrink = jnp.exp2(old - new)
        m_s[yq] = new
        l_s[yq] = l_s[yq] * shrink + jnp.sum(weights, axis=0, keepdims=True)
        acc[yq] = acc[yq] * shrink + jnp.dot(
            vt, weights.astype(jnp.bfloat16), preferred_element_type=jnp.float32
        )

    def compute(e):
        s, yk = e // 4, (e + 3) % 4
        zz = place(s)
        landed(kv.at[1 - c, zz, yk], h_r.at[s, yk])
        need_mask = (yk == 3) | (zz == z)

        def later(yq, _):
            attend(yq, zz, yk, False)
            return 0

        first = jnp.where((zz < z) & (yk < 3), yk, yk + 1)
        lax.fori_loop(first, 3, later, 0)

        @pl.when(need_mask & (zz <= z))
        def _():
            attend(yk, zz, yk, True)

    for e in range(4):
        comm(e)
    for yy in range(4):
        for xx in range(2):
            landed(q_in.at[yy, xx], q_r.at[yy, xx])
            scaled = q_in[yy, xx].astype(jnp.float32) * QSCALE
            hi = scaled.astype(jnp.bfloat16)
            qt[yy, :HD, xx * T:(xx + 1) * T] = hi
            qt[yy, HD:, xx * T:(xx + 1) * T] = (scaled - hi.astype(jnp.float32)).astype(jnp.bfloat16)

    def turn(e, _):
        @pl.when(e < 32)
        def _():
            comm(e)

        compute(e - 4)
        return 0

    lax.fori_loop(4, 36, turn, 0)

    def back(yy, xx):
        j = 2 * (y % 2) + c
        to = dev(yy, z, xx, y // 2)
        return (
            remote(o_out.at[yy, xx], o_in.at[x, j], ot_s.at[yy, xx], ot_r.at[x, j], to),
            remote(st_out.at[yy, xx], st_in.at[x, j], st_s.at[yy, xx], st_r.at[x, j], to),
        )

    def back_self(yy, xx):
        return (yy == y) & (xx == x) & (c == y // 2)

    def back_here(yy, xx):
        j = 2 * (y % 2) + c
        pltpu.make_async_copy(o_out.at[yy, xx], o_in.at[x, j], ot_r.at[x, j]).start()
        pltpu.make_async_copy(st_out.at[yy, xx], st_in.at[x, j], st_r.at[x, j]).start()

    for yy in (3, 0, 1, 2):
        part = acc[yy] / l_s[yy]
        for xx in range(2):
            lanes = slice(xx * T, (xx + 1) * T)
            o_out[yy, xx] = part[:, lanes].astype(jnp.bfloat16)
            st_out[yy, xx, 0:1] = m_s[yy][:, lanes]
            st_out[yy, xx, 1:2] = l_s[yy][:, lanes]
            st_out[yy, xx, 2:8] = jnp.zeros((6, T), jnp.float32)
            either(
                back_self(yy, xx),
                lambda yy=yy, xx=xx: [copy.start() for copy in back(yy, xx)],
                lambda yy=yy, xx=xx: back_here(yy, xx),
            )

    for j in range(4):
        for xx in range(2):
            landed(o_in.at[xx, j], ot_r.at[xx, j])
            landed(st_in.at[xx, j], st_r.at[xx, j])
        m0, m1 = st_in[0, j, 0:1], st_in[1, j, 0:1]
        peak = jnp.maximum(m0, m1)
        a0 = st_in[0, j, 1:2] * jnp.exp2(m0 - peak)
        a1 = st_in[1, j, 1:2] * jnp.exp2(m1 - peak)
        whole = a0 + a1
        merged = o_in[0, j].astype(jnp.float32) * (a0 / whole) + o_in[1, j].astype(jnp.float32) * (
            a1 / whole
        )
        att[:, j * HD:(j + 1) * HD] = merged.T.astype(jnp.bfloat16)

    w_copy.wait()

    def to_sib(n):
        return remote(p_sib.at[n], sib_in.at[n], sb_s.at[n], sb_r.at[n], dev(y, z, x, 1 - c))

    def to_cut(n):
        return remote(cut_out.at[n], cut_in.at[n], cu_s.at[n], cu_r.at[n], dev(y, z, x, c, 1 - xh))

    def project(n):
        cols = pl.ds(pl.multiple_of(n * CH, CH), CH)
        part = jnp.dot(att[...], w_vm[:, cols], preferred_element_type=jnp.float32)
        for h in range(4):
            rows = part[64 * h:64 * (h + 1)]

            @pl.when(c == h % 2)
            def _():
                p_own[n, h // 2] = rows

            @pl.when(c != h % 2)
            def _():
                p_sib[n, h // 2] = rows.astype(jnp.bfloat16)

        to_sib(n).start()

    def reduce_chip(n):
        to_sib(n).wait_recv()
        cut_out[n] = (p_own[n, 1 - xh] + sib_in[n, 1 - xh].astype(jnp.float32)).astype(jnp.bfloat16)
        to_cut(n).start()

    def proj_turn(n, _):
        @pl.when(n < NCH)
        def _():
            project(n)

        @pl.when(n > 0)
        def _():
            reduce_chip(n - 1)

        return 0

    lax.fori_loop(0, NCH + 1, proj_turn, 0)
    for n in range(NCH):
        to_cut(n).wait_recv()
        total = p_own[n, xh] + sib_in[n, xh].astype(jnp.float32) + cut_in[n].astype(jnp.float32)
        o_ref[:, n * CH:(n + 1) * CH] = total.astype(jnp.bfloat16)

    for i in range(2):
        for n in range(2):
            either(kv_self(i, n), lambda i=i, n=n: kv_copy(i, n).wait_send(), None)
    for j in range(4):
        for xx in range(2):
            either(q_self(j, xx), lambda j=j, xx=xx: q_copy(j, xx).wait_send(), None)

    def drain(e, _):
        s, yk = e // 4, (e + 3) % 4
        forwards(s, yk, lambda copy: copy.wait_send())
        share(s, yk).wait_send()
        return 0

    lax.fori_loop(0, 32, drain, 0)
    for yy in range(4):
        for xx in range(2):
            either(
                back_self(yy, xx),
                lambda yy=yy, xx=xx: [copy.wait_send() for copy in back(yy, xx)],
                None,
            )
    for n in range(NCH):
        to_sib(n).wait_send()
        to_cut(n).wait_send()


def per_device(queries, keys, values, doc_ids, out_weight):
    bf, f32 = jnp.bfloat16, jnp.float32
    vm, dma = pltpu.VMEM, pltpu.SemaphoreType.DMA
    scratch = [
        vm((512, D), bf),
        vm((4, HD, T), bf),
        vm((2, 2, T, HD), bf),
        vm((2, NZ, NY, T, HD), bf),
        vm((NY, NX, HD, T), bf),
        vm((NY, 2 * HD, 2 * T), bf),
        vm((NY, 1, 2 * T), f32),
        vm((NY, 1, 2 * T), f32),
        vm((NY, HD, 2 * T), f32),
        vm((NY, NX, HD, T), bf),
        vm((NY, NX, 8, T), f32),
        vm((NX, 4, HD, T), bf),
        vm((NX, 4, 8, T), f32),
        vm((T, 512), bf),
        vm((NCH, 2, 64, CH), f32),
        vm((NCH, 2, 64, CH), bf),
        vm((NCH, 2, 64, CH), bf),
        vm((NCH, 64, CH), bf),
        vm((NCH, 64, CH), bf),
        dma,
        dma((2, 2)),
        dma((4, 2)),
        dma((8, 4)),
        dma((8, 4)),
        dma((8, 4)),
        dma((8, 4)),
        dma((4, 2)),
        dma((4, 2)),
        dma((2, 4)),
        dma((4, 2)),
        dma((2, 4)),
        dma((NCH,)),
        dma((NCH,)),
        dma((NCH,)),
        dma((NCH,)),
    ]
    vmem = pl.BlockSpec(memory_space=pltpu.VMEM)
    return pl.pallas_call(
        kernel,
        out_shape=jax.ShapeDtypeStruct((64, D), bf),
        in_specs=[
            vmem, vmem, vmem,
            pl.BlockSpec(memory_space=pltpu.SMEM),
            pl.BlockSpec(memory_space=pl.ANY),
        ],
        out_specs=vmem,
        scratch_shapes=scratch,
        compiler_params=pltpu.CompilerParams(
            collective_id=0, has_side_effects=True, vmem_limit_bytes=48 * 2**20
        ),
    )(queries, keys, values, doc_ids, out_weight)


def solution(mesh):
    placed = (P("ctx", "head"), P("ctx", "head"), P("ctx", "head"), P(), P("head", None))
    return jax.shard_map(
        per_device, mesh=mesh, in_specs=placed, out_specs=P(("ctx", "head"), None), check_vma=False
    )
```

```python
import functools

import jax
import jax.numpy as jnp
import numpy as np
from jax import lax
from jax.experimental import pallas as pl
from jax.experimental.pallas import tpu as pltpu
from jax.sharding import PartitionSpec as P

MESH = pl.DeviceIdType.MESH
HD = 128
T = 256
NY, NZ, NX = 4, 8, 2
D = 5376
CH = 768
NCH = D // CH
QSCALE = float(168.0 ** (-0.5) * np.log2(np.e))
NEG = -1e30


def kernel(
    q_hbm, k_hbm, v_hbm, doc_hbm, w_ref, o_ref, q_ref, k_ref, v_ref, doc_ref,
    w_vm, qsrc, ksrc, kv, q_in, qt, m_s, l_s, acc, o_out, st_out, o_in, st_in,
    att, p_own, p_sib, sib_in, cut_out, cut_in,
    in_s, w_sem, a_kv_s, a_q_s, r_sem, f_sem, h_s, h_r, q_r, ot_s, ot_r, st_s, st_r,
    sb_s, sb_r, cu_s, cu_r,
):
    ctx, head = lax.axis_index("ctx"), lax.axis_index("head")
    y, z, x = ctx // 16, (ctx // 2) % 8, ctx % 2
    xh, c = head // 2, head % 2

    def dev(yy, zz, xx, cc, hh=xh):
        return {"ctx": (yy * 8 + zz) * 2 + xx, "head": hh * 2 + cc}

    def remote(src, dst, s, r, to):
        return pltpu.make_async_remote_copy(
            src_ref=src, dst_ref=dst, send_sem=s, recv_sem=r, device_id=to, device_id_type=MESH
        )

    loads = [
        pltpu.make_async_copy(src, dst, in_s.at[i])
        for i, (src, dst) in enumerate(
            ((q_hbm, q_ref), (k_hbm, k_ref), (v_hbm, v_ref), (doc_hbm, doc_ref))
        )
    ]
    for load in loads:
        load.start()
    barrier = pltpu.get_barrier_semaphore()

    def greet(to):
        pl.semaphore_signal(barrier, inc=1, device_id=to, device_id_type=MESH)

    for i in range(1, 16):
        greet(dev((y + i // 4) % 4, z, (x + (i // 2) % 2) % 2, (c + i) % 2))
    up, down = (z + 1) % 8, (z + 7) % 8
    greet(dev(y, up, x, c))
    greet(dev(y, down, x, c))
    greet(dev(y, z, x, c, 1 - xh))

    w_copy = pltpu.make_async_copy(w_ref, w_vm, w_sem)
    w_copy.start()

    for load in loads:
        load.wait()
    for i in range(2):
        ksrc[0, i] = k_ref[:, i * HD:(i + 1) * HD]
        for t in range(2):
            part = v_ref[t * HD:(t + 1) * HD, i * HD:(i + 1) * HD]
            ksrc[1, i, t * HD:(t + 1) * HD, :] = part.astype(jnp.float32).T.astype(jnp.bfloat16)
    for j in range(4):
        part = q_ref[:, j * HD:(j + 1) * HD]
        qsrc[j] = part.astype(jnp.float32).T.astype(jnp.bfloat16)
    m_s[...] = jnp.full(m_s.shape, NEG, jnp.float32)
    l_s[...] = jnp.zeros(l_s.shape, jnp.float32)
    acc[...] = jnp.zeros(acc.shape, jnp.float32)

    pl.semaphore_wait(barrier, 18)

    def kv_copy(i, n):
        return remote(
            ksrc.at[n, i], kv.at[n, z, y], a_kv_s.at[n, i], r_sem.at[0, y], dev(2 * c + i, z, x, n)
        )

    def kv_self(i, n):
        return (2 * c + i == y) & (c == n)

    def q_copy(j, xx):
        return remote(
            qsrc.at[j], q_in.at[y, x], a_q_s.at[j, xx], q_r.at[y, x],
            dev(2 * c + j // 2, z, xx, j % 2),
        )

    def q_self(j, xx):
        return (2 * c + j // 2 == y) & (c == j % 2) & (xx == x)

    def either(cond, there, here):
        @pl.when(jnp.logical_not(cond))
        def _():
            there()

        if here is not None:

            @pl.when(cond)
            def _():
                here()

    for i in range(2):
        for n in range(2):
            either(
                kv_self(i, n),
                lambda i=i, n=n: kv_copy(i, n).start(),
                lambda i=i, n=n: pltpu.make_async_copy(
                    ksrc.at[n, i], kv.at[n, z, y], r_sem.at[0, y]
                ).start(),
            )
    def place(s):
        dist = (s + 1) // 2
        return (z + 8 + jnp.where(s % 2 == 1, -dist, dist)) % 8

    def pass_on(s, yk, to_slot, to_z):
        zz = place(s)
        return remote(
            kv.at[c, zz, yk], kv.at[c, zz, yk], f_sem.at[to_slot, yk], r_sem.at[to_slot, yk],
            dev(y, to_z, x, c),
        )

    def share(s, yk):
        zz = place(s)
        return remote(
            kv.at[c, zz, yk], kv.at[c, zz, yk], h_s.at[s, yk], h_r.at[s, yk], dev(y, z, x, 1 - c)
        )

    def landed(ref, sem):
        pltpu.make_async_copy(ref, ref, sem).wait()

    def forwards(s, yk, act):
        @pl.when(s == 0)
        def _():
            act(pass_on(s, yk, 1, up))
            act(pass_on(s, yk, 2, down))

        @pl.when((s > 0) & (s < 5))
        def _():
            act(pass_on(s, yk, s + 2, jnp.where(s % 2 == 1, up, down)))

        @pl.when((s == 5) & (c == 0))
        def _():
            act(pass_on(s, yk, 7, up))

        @pl.when((s == 6) & (c == 1))
        def _():
            act(pass_on(s, yk, 7, down))

    order = (3, 0, 1, 2)

    def arrive(s, yk):
        landed(kv.at[c, place(s), yk], r_sem.at[s, yk])
        forwards(s, yk, lambda copy: copy.start())
        share(s, yk).start()

    def event(e, _):
        s, yk = 2 * (e // 4) + 1, (e + 3) % 4
        arrive(s, yk)

        @pl.when(s < 7)
        def _():
            arrive(s + 1, yk)

        return 0

    def scores_of(yq, zz, yk, masked):
        kb = kv[0, zz, yk]
        scores = jnp.dot(
            jnp.concatenate([kb, kb], axis=1), qt[yq], preferred_element_type=jnp.float32
        )
        if masked:
            row = lax.broadcasted_iota(jnp.int32, (T, 1), 0)
            col = lax.broadcasted_iota(jnp.int32, (1, 2 * T), 1)
            kbase, qbase = (16 * yk + 2 * zz + x) * 2, (16 * yq + 2 * z) * 2
            kdoc = jnp.where(row < HD, doc_ref[kbase], doc_ref[kbase + 1])
            qdoc = jnp.where(
                col < HD, doc_ref[qbase],
                jnp.where(
                    col < 2 * HD, doc_ref[qbase + 1],
                    jnp.where(col < 3 * HD, doc_ref[qbase + 2], doc_ref[qbase + 3]),
                ),
            )
            allowed = (kdoc == qdoc) & (row + kbase * HD <= col + qbase * HD)
            scores = jnp.where(allowed, scores, NEG)
        return scores

    def soften(yq, scores):
        old = m_s[yq]
        new = jnp.maximum(old, jnp.max(scores, axis=0, keepdims=True))
        m_s[yq] = new
        return jnp.exp2(scores - new).astype(jnp.bfloat16), jnp.exp2(old - new)

    def add_values(yq, zz, yk, weights, shrink):
        vb = kv[1, zz, yk]
        vt = jnp.concatenate([vb[:HD], vb[HD:]], axis=1)
        vt = jnp.concatenate([vt, jnp.ones((16, T), jnp.bfloat16)], axis=0)
        added = jnp.dot(vt, weights, preferred_element_type=jnp.float32)
        l_s[yq] = l_s[yq] * shrink + added[HD:HD + 1]
        acc[yq] = acc[yq] * shrink + added[:HD]

    def attend(zz, pieces):
        scores = [scores_of(yq, zz, yk, masked) for yq, yk, masked in pieces]
        soft = [soften(piece[0], one) for piece, one in zip(pieces, scores)]
        for (yq, yk, _), (weights, shrink) in zip(pieces, soft):
            add_values(yq, zz, yk, weights, shrink)

    before = [(2, 0, False), (1, 0, False), (2, 1, False)]

    def compute(s):
        zz = place(s)
        for yk in order:
            landed(kv.at[1 - c, zz, yk], h_r.at[s, yk])

        @pl.when(zz > z)
        def _():
            attend(zz, before)

        @pl.when(zz < z)
        def _():
            attend(zz, before + [(0, 0, False), (2, 2, False), (1, 1, False), (3, 3, True)])

        @pl.when(zz == z)
        def _():
            attend(zz, before + [(0, 0, True), (2, 2, True), (1, 1, True), (3, 3, True)])

    def send_queries():
        for j in range(4):
            for xx in range(2):
                either(
                    q_self(j, xx),
                    lambda j=j, xx=xx: q_copy(j, xx).start(),
                    lambda j=j, xx=xx: pltpu.make_async_copy(
                        qsrc.at[j], q_in.at[y, x], q_r.at[y, x]
                    ).start(),
                )

    for n, yk in enumerate(order):
        arrive(0, yk)
    send_queries()
    lax.fori_loop(0, 4, event, 0)
    for yy in range(4):
        for xx in range(2):
            landed(q_in.at[yy, xx], q_r.at[yy, xx])
            scaled = q_in[yy, xx].astype(jnp.float32) * QSCALE
            hi = scaled.astype(jnp.bfloat16)
            qt[yy, :HD, xx * T:(xx + 1) * T] = hi
            qt[yy, HD:, xx * T:(xx + 1) * T] = (scaled - hi.astype(jnp.float32)).astype(jnp.bfloat16)

    def seen(n):
        first = jnp.where(n < 1, 0, jnp.where(n < 5, n + 1, 8))
        return 4 + jnp.where(n < 6, first, jnp.where(n < 7, 9, 12))

    def turn(n, _):
        lax.fori_loop(jnp.where(n < 1, 4, seen(n - 1)), seen(n), event, 0)
        compute(n)
        return 0

    lax.fori_loop(0, 8, turn, 0)

    halves = (1 - xh, xh)

    def back(yy, xx, n):
        j = 2 * (y % 2) + c
        return remote(
            o_out.at[yy, xx, halves[n]], o_in.at[x, j, halves[n]],
            ot_s.at[n, yy, xx], ot_r.at[n, x, j], dev(yy, z, xx, y // 2),
        )

    def back_stats(yy, xx):
        j = 2 * (y % 2) + c
        return remote(
            st_out.at[yy, xx], st_in.at[x, j], st_s.at[yy, xx], st_r.at[x, j],
            dev(yy, z, xx, y // 2),
        )

    def back_self(yy, xx):
        return (yy == y) & (xx == x) & (c == y // 2)

    def back_here(yy, xx, n):
        j = 2 * (y % 2) + c
        pltpu.make_async_copy(
            o_out.at[yy, xx, halves[n]], o_in.at[x, j, halves[n]], ot_r.at[n, x, j]
        ).start()

    def back_stats_here(yy, xx):
        j = 2 * (y % 2) + c
        pltpu.make_async_copy(st_out.at[yy, xx], st_in.at[x, j], st_r.at[x, j]).start()

    def return_half(yy, xx, n):
        either(
            back_self(yy, xx),
            lambda: back(yy, xx, n).start(),
            lambda: back_here(yy, xx, n),
        )

    for yy in order:
        part = (acc[yy] * (1.0 / l_s[yy])).astype(jnp.bfloat16)
        for xx in range(2):
            for th in range(2):
                lanes = slice(xx * T + th * HD, xx * T + (th + 1) * HD)
                o_out[yy, xx, th] = part[:, lanes]
                st_out[yy, xx, th, 0:1] = m_s[yy][:, lanes]
                st_out[yy, xx, th, 1:2] = l_s[yy][:, lanes]
                st_out[yy, xx, th, 2:8] = jnp.zeros((6, HD), jnp.float32)
            either(
                back_self(yy, xx),
                lambda yy=yy, xx=xx: back_stats(yy, xx).start(),
                lambda yy=yy, xx=xx: back_stats_here(yy, xx),
            )
            return_half(yy, xx, 0)
    for yy in order:
        for xx in range(2):
            return_half(yy, xx, 1)

    def merge(n):
        for j in range(4):
            for xx in range(2):
                landed(o_in.at[xx, j, halves[n]], ot_r.at[n, xx, j])
                if n == 0:
                    landed(st_in.at[xx, j], st_r.at[xx, j])
            one, two = st_in[0, j, halves[n]], st_in[1, j, halves[n]]
            peak = jnp.maximum(one[0:1], two[0:1])
            a0 = one[1:2] * jnp.exp2(one[0:1] - peak)
            a1 = two[1:2] * jnp.exp2(two[0:1] - peak)
            whole = a0 + a1
            merged = o_in[0, j, halves[n]].astype(jnp.float32) * (a0 / whole) + o_in[
                1, j, halves[n]
            ].astype(jnp.float32) * (a1 / whole)
            att[n, :, j * HD:(j + 1) * HD] = merged.T.astype(jnp.bfloat16)

    def to_sib(h, n):
        return remote(
            p_sib.at[h, n], sib_in.at[h, n], sb_s.at[h, n], sb_r.at[h, n], dev(y, z, x, 1 - c)
        )

    def to_cut(n):
        return remote(cut_out.at[n], cut_in.at[n], cu_s.at[n], cu_r.at[n], dev(y, z, x, c, 1 - xh))

    def project(h, n):
        cols = pl.ds(pl.multiple_of(n * CH, CH), CH)
        part = jnp.dot(att[h], w_vm[:, cols], preferred_element_type=jnp.float32)

        @pl.when(c == 0)
        def _():
            p_own[h, n] = part[:64]
            p_sib[h, n] = part[64:].astype(jnp.bfloat16)

        @pl.when(c == 1)
        def _():
            p_own[h, n] = part[64:]
            p_sib[h, n] = part[:64].astype(jnp.bfloat16)

        to_sib(h, n).start()

    def reduce_chip(n):
        to_sib(0, n).wait_recv()
        cut_out[n] = (p_own[0, n] + sib_in[0, n].astype(jnp.float32)).astype(jnp.bfloat16)
        to_cut(n).start()

    def first_turn(n, _):
        @pl.when(n < NCH)
        def _():
            project(0, n)

        @pl.when(n > 0)
        def _():
            reduce_chip(n - 1)

        return 0

    def second_turn(n, _):
        project(1, n)
        return 0

    merge(0)
    w_copy.wait()
    lax.fori_loop(0, NCH + 1, first_turn, 0)
    merge(1)
    lax.fori_loop(0, NCH, second_turn, 0)
    for n in range(NCH):
        to_sib(1, n).wait_recv()
        p_own[1, n] = p_own[1, n] + sib_in[1, n].astype(jnp.float32)
    for n in range(NCH):
        to_cut(n).wait_recv()
        total = p_own[1, n] + cut_in[n].astype(jnp.float32)
        o_ref[:, n * CH:(n + 1) * CH] = total.astype(jnp.bfloat16)

    for i in range(2):
        for n in range(2):
            either(kv_self(i, n), lambda i=i, n=n: kv_copy(i, n).wait_send(), None)
    for j in range(4):
        for xx in range(2):
            either(q_self(j, xx), lambda j=j, xx=xx: q_copy(j, xx).wait_send(), None)

    for yk in order:
        forwards(0, yk, lambda copy: copy.wait_send())
    for yk in order:
        share(0, yk).wait_send()

    def drain(s, _):
        for yk in order:
            forwards(s, yk, lambda copy: copy.wait_send())
            share(s, yk).wait_send()
        return 0

    lax.fori_loop(1, 8, drain, 0)
    for yy in range(4):
        for xx in range(2):
            either(
                back_self(yy, xx),
                lambda yy=yy, xx=xx: [
                    copy.wait_send()
                    for copy in (back_stats(yy, xx), back(yy, xx, 0), back(yy, xx, 1))
                ],
                None,
            )
    for n in range(NCH):
        to_sib(0, n).wait_send()
        to_sib(1, n).wait_send()
        to_cut(n).wait_send()


def per_device(queries, keys, values, doc_ids, out_weight):
    bf, f32 = jnp.bfloat16, jnp.float32
    vm, dma = pltpu.VMEM, pltpu.SemaphoreType.DMA
    scratch = [
        vm((T, 512), bf),
        vm((T, 256), bf),
        vm((T, 256), bf),
        pltpu.SMEM((128,), jnp.int32),
        vm((512, D), bf),
        vm((4, HD, T), bf),
        vm((2, 2, T, HD), bf),
        vm((2, NZ, NY, T, HD), bf),
        vm((NY, NX, HD, T), bf),
        vm((NY, 2 * HD, 2 * T), bf),
        vm((NY, 1, 2 * T), f32),
        vm((NY, 1, 2 * T), f32),
        vm((NY, HD, 2 * T), f32),
        vm((NY, NX, 2, HD, HD), bf),
        vm((NY, NX, 2, 8, HD), f32),
        vm((NX, 4, 2, HD, HD), bf),
        vm((NX, 4, 2, 8, HD), f32),
        vm((2, HD, 512), bf),
        vm((2, NCH, 64, CH), f32),
        vm((2, NCH, 64, CH), bf),
        vm((2, NCH, 64, CH), bf),
        vm((NCH, 64, CH), bf),
        vm((NCH, 64, CH), bf),
        dma((4,)),
        dma,
        dma((2, 2)),
        dma((4, 2)),
        dma((8, 4)),
        dma((8, 4)),
        dma((8, 4)),
        dma((8, 4)),
        dma((4, 2)),
        dma((2, 4, 2)),
        dma((2, 2, 4)),
        dma((4, 2)),
        dma((2, 4)),
        dma((2, NCH)),
        dma((2, NCH)),
        dma((NCH,)),
        dma((NCH,)),
    ]
    vmem = pl.BlockSpec(memory_space=pltpu.VMEM)
    return pl.pallas_call(
        kernel,
        out_shape=jax.ShapeDtypeStruct((64, D), bf),
        in_specs=[pl.BlockSpec(memory_space=pltpu.HBM)] * 5,
        out_specs=vmem,
        scratch_shapes=scratch,
        compiler_params=pltpu.CompilerParams(
            collective_id=0, has_side_effects=True, vmem_limit_bytes=64 * 2**20
        ),
    )(queries, keys, values, doc_ids, out_weight)


def solution(mesh):
    placed = (P("ctx", "head"), P("ctx", "head"), P("ctx", "head"), P(), P("head", None))
    return jax.shard_map(
        per_device, mesh=mesh, in_specs=placed, out_specs=P(("ctx", "head"), None), check_vma=False
    )
```

```python
import functools

import jax
import jax.numpy as jnp
import numpy as np
from jax import lax
from jax.experimental import pallas as pl
from jax.experimental.pallas import tpu as pltpu
from jax.sharding import PartitionSpec as P

MESH = pl.DeviceIdType.MESH
HD = 128
T = 256
NY, NZ, NX = 4, 8, 2
D = 5376
CH = 768
NCH = D // CH
QSCALE = float(168.0 ** (-0.5) * np.log2(np.e))
NEG = -1e30


def kernel(
    q_hbm, k_hbm, v_hbm, doc_hbm, w_ref, o_ref, q_ref, k_ref, v_ref, doc_ref,
    w_vm, qsrc, ksrc, kv, q_in, qt, m_s, l_s, acc, o_out, st_out, o_in, st_in,
    att, p_own, p_sib, sib_in, cut_out, cut_in, out_vm,
    in_s, out_s, w_sem, a_kv_s, a_q_s, r_sem, f_sem, h_s, h_r, q_r, ot_s, ot_r, st_s, st_r,
    sb_s, sb_r, cu_s, cu_r,
):
    ctx, head = lax.axis_index("ctx"), lax.axis_index("head")
    y, z, x = ctx // 16, (ctx // 2) % 8, ctx % 2
    xh, c = head // 2, head % 2

    def dev(yy, zz, xx, cc, hh=xh):
        return {"ctx": (yy * 8 + zz) * 2 + xx, "head": hh * 2 + cc}

    def remote(src, dst, s, r, to):
        return pltpu.make_async_remote_copy(
            src_ref=src, dst_ref=dst, send_sem=s, recv_sem=r, device_id=to, device_id_type=MESH
        )

    loads = [
        pltpu.make_async_copy(src, dst, in_s.at[i])
        for i, (src, dst) in enumerate(
            ((q_hbm, q_ref), (k_hbm, k_ref), (v_hbm, v_ref), (doc_hbm, doc_ref))
        )
    ]
    for load in loads:
        load.start()
    barrier = pltpu.get_barrier_semaphore()

    def greet(to):
        pl.semaphore_signal(barrier, inc=1, device_id=to, device_id_type=MESH)

    for i in range(1, 16):
        greet(dev((y + i // 4) % 4, z, (x + (i // 2) % 2) % 2, (c + i) % 2))
    up, down = (z + 1) % 8, (z + 7) % 8
    greet(dev(y, up, x, c))
    greet(dev(y, down, x, c))
    greet(dev(y, z, x, c, 1 - xh))

    w_copy = pltpu.make_async_copy(w_ref, w_vm, w_sem)
    w_copy.start()

    for load in loads:
        load.wait()
    for i in range(2):
        ksrc[0, i] = k_ref[:, i * HD:(i + 1) * HD]
        for t in range(2):
            part = v_ref[t * HD:(t + 1) * HD, i * HD:(i + 1) * HD]
            ksrc[1, i, t * HD:(t + 1) * HD, :] = part.astype(jnp.float32).T.astype(jnp.bfloat16)
    for j in range(4):
        part = q_ref[:, j * HD:(j + 1) * HD]
        qsrc[j] = part.astype(jnp.float32).T.astype(jnp.bfloat16)
    m_s[...] = jnp.full(m_s.shape, NEG, jnp.float32)
    l_s[...] = jnp.zeros(l_s.shape, jnp.float32)
    acc[...] = jnp.zeros(acc.shape, jnp.float32)

    pl.semaphore_wait(barrier, 18)

    def kv_copy(i, n):
        return remote(
            ksrc.at[n, i], kv.at[n, z, y], a_kv_s.at[n, i], r_sem.at[0, y], dev(2 * c + i, z, x, n)
        )

    def kv_self(i, n):
        return (2 * c + i == y) & (c == n)

    def q_copy(j, xx):
        return remote(
            qsrc.at[j], q_in.at[y, x], a_q_s.at[j, xx], q_r.at[y, x],
            dev(2 * c + j // 2, z, xx, j % 2),
        )

    def q_self(j, xx):
        return (2 * c + j // 2 == y) & (c == j % 2) & (xx == x)

    def either(cond, there, here):
        @pl.when(jnp.logical_not(cond))
        def _():
            there()

        if here is not None:

            @pl.when(cond)
            def _():
                here()

    for i in range(2):
        for n in range(2):
            either(
                kv_self(i, n),
                lambda i=i, n=n: kv_copy(i, n).start(),
                lambda i=i, n=n: pltpu.make_async_copy(
                    ksrc.at[n, i], kv.at[n, z, y], r_sem.at[0, y]
                ).start(),
            )
    def place(s):
        dist = (s + 1) // 2
        return (z + 8 + jnp.where(s % 2 == 1, -dist, dist)) % 8

    def pass_on(s, yk, to_slot, to_z):
        zz = place(s)
        return remote(
            kv.at[c, zz, yk], kv.at[c, zz, yk], f_sem.at[to_slot, yk], r_sem.at[to_slot, yk],
            dev(y, to_z, x, c),
        )

    def share(s, yk):
        zz = place(s)
        return remote(
            kv.at[c, zz, yk], kv.at[c, zz, yk], h_s.at[s, yk], h_r.at[s, yk], dev(y, z, x, 1 - c)
        )

    def landed(ref, sem):
        pltpu.make_async_copy(ref, ref, sem).wait()

    def forwards(s, yk, act):
        @pl.when(s == 0)
        def _():
            act(pass_on(s, yk, 1, up))
            act(pass_on(s, yk, 2, down))

        @pl.when((s > 0) & (s < 5))
        def _():
            act(pass_on(s, yk, s + 2, jnp.where(s % 2 == 1, up, down)))

        @pl.when((s == 5) & (c == 0))
        def _():
            act(pass_on(s, yk, 7, up))

        @pl.when((s == 6) & (c == 1))
        def _():
            act(pass_on(s, yk, 7, down))

    order = (3, 0, 1, 2)

    def arrive(s, yk):
        landed(kv.at[c, place(s), yk], r_sem.at[s, yk])
        forwards(s, yk, lambda copy: copy.start())
        share(s, yk).start()

    def chunk(n):
        return (y + n + (n == 2) * 1 - (n == 3) * 1) % 4

    def event(e, _):
        n = e % 4
        s, yk = 2 * (e // 4) + 1, (y + n + jnp.where(n == 2, 1, jnp.where(n == 3, -1, 0))) % 4
        arrive(s, yk)

        @pl.when(s < 7)
        def _():
            arrive(s + 1, yk)

        return 0

    def scores_of(yq, zz, yk, masked):
        kb = kv[0, zz, yk]
        scores = jnp.dot(
            jnp.concatenate([kb, kb], axis=1), qt[yq], preferred_element_type=jnp.float32
        )
        if masked:
            row = lax.broadcasted_iota(jnp.int32, (T, 1), 0)
            col = lax.broadcasted_iota(jnp.int32, (1, 2 * T), 1)
            kbase, qbase = (16 * yk + 2 * zz + x) * 2, (16 * yq + 2 * z) * 2
            kdoc = jnp.where(row < HD, doc_ref[kbase], doc_ref[kbase + 1])
            qdoc = jnp.where(
                col < HD, doc_ref[qbase],
                jnp.where(
                    col < 2 * HD, doc_ref[qbase + 1],
                    jnp.where(col < 3 * HD, doc_ref[qbase + 2], doc_ref[qbase + 3]),
                ),
            )
            allowed = (kdoc == qdoc) & (row + kbase * HD <= col + qbase * HD)
            scores = jnp.where(allowed, scores, NEG)
        return scores

    def soften(yq, scores):
        old = m_s[yq]
        new = jnp.maximum(old, jnp.max(scores, axis=0, keepdims=True))
        m_s[yq] = new
        return jnp.exp2(scores - new).astype(jnp.bfloat16), jnp.exp2(old - new)

    def add_values(yq, zz, yk, weights, shrink):
        vb = kv[1, zz, yk]
        vt = jnp.concatenate([vb[:HD], vb[HD:]], axis=1)
        vt = jnp.concatenate([vt, jnp.ones((16, T), jnp.bfloat16)], axis=0)
        added = jnp.dot(vt, weights, preferred_element_type=jnp.float32)
        l_s[yq] = l_s[yq] * shrink + added[HD:HD + 1]
        acc[yq] = acc[yq] * shrink + added[:HD]

    def attend(zz, pieces):
        scores = [scores_of(yq, zz, yk, masked) for yq, yk, masked in pieces]
        soft = [soften(piece[0], one) for piece, one in zip(pieces, scores)]
        for (yq, yk, _), (weights, shrink) in zip(pieces, soft):
            add_values(yq, zz, yk, weights, shrink)

    before = [(2, 0, False), (1, 0, False), (2, 1, False)]

    def compute(s):
        zz = place(s)
        for yk in order:
            landed(kv.at[1 - c, zz, yk], h_r.at[s, yk])

        @pl.when(zz > z)
        def _():
            attend(zz, before)

        @pl.when(zz < z)
        def _():
            attend(zz, before + [(0, 0, False), (2, 2, False), (1, 1, False), (3, 3, True)])

        @pl.when(zz == z)
        def _():
            attend(zz, before + [(0, 0, True), (2, 2, True), (1, 1, True), (3, 3, True)])

    def send_queries():
        for j in range(4):
            for xx in range(2):
                either(
                    q_self(j, xx),
                    lambda j=j, xx=xx: q_copy(j, xx).start(),
                    lambda j=j, xx=xx: pltpu.make_async_copy(
                        qsrc.at[j], q_in.at[y, x], q_r.at[y, x]
                    ).start(),
                )

    for n in range(4):
        arrive(0, chunk(n))
    send_queries()
    lax.fori_loop(0, 4, event, 0)
    for yy in range(4):
        for xx in range(2):
            landed(q_in.at[yy, xx], q_r.at[yy, xx])
            scaled = q_in[yy, xx].astype(jnp.float32) * QSCALE
            hi = scaled.astype(jnp.bfloat16)
            qt[yy, :HD, xx * T:(xx + 1) * T] = hi
            qt[yy, HD:, xx * T:(xx + 1) * T] = (scaled - hi.astype(jnp.float32)).astype(jnp.bfloat16)

    def seen(n):
        first = jnp.where(n < 1, 0, jnp.where(n < 5, n + 1, 8))
        return 4 + jnp.where(n < 6, first, jnp.where(n < 7, 9, 12))

    def turn(n, _):
        lax.fori_loop(jnp.where(n < 1, 4, seen(n - 1)), seen(n), event, 0)
        compute(n)
        return 0

    lax.fori_loop(0, 8, turn, 0)

    halves = (1 - xh, xh)

    def back(yy, xx, n):
        j = 2 * (y % 2) + c
        return remote(
            o_out.at[yy, xx, halves[n]], o_in.at[x, j, halves[n]],
            ot_s.at[n, yy, xx], ot_r.at[n, x, j], dev(yy, z, xx, y // 2),
        )

    def back_stats(yy, xx):
        j = 2 * (y % 2) + c
        return remote(
            st_out.at[yy, xx], st_in.at[x, j], st_s.at[yy, xx], st_r.at[x, j],
            dev(yy, z, xx, y // 2),
        )

    def back_self(yy, xx):
        return (yy == y) & (xx == x) & (c == y // 2)

    def back_here(yy, xx, n):
        j = 2 * (y % 2) + c
        pltpu.make_async_copy(
            o_out.at[yy, xx, halves[n]], o_in.at[x, j, halves[n]], ot_r.at[n, x, j]
        ).start()

    def back_stats_here(yy, xx):
        j = 2 * (y % 2) + c
        pltpu.make_async_copy(st_out.at[yy, xx], st_in.at[x, j], st_r.at[x, j]).start()

    def return_half(yy, xx, n):
        either(
            back_self(yy, xx),
            lambda: back(yy, xx, n).start(),
            lambda: back_here(yy, xx, n),
        )

    for yy in order:
        part = (acc[yy] * (1.0 / l_s[yy])).astype(jnp.bfloat16)
        for xx in range(2):
            for th in range(2):
                lanes = slice(xx * T + th * HD, xx * T + (th + 1) * HD)
                o_out[yy, xx, th] = part[:, lanes]
                st_out[yy, xx, th, 0:1] = m_s[yy][:, lanes]
                st_out[yy, xx, th, 1:2] = l_s[yy][:, lanes]
                st_out[yy, xx, th, 2:8] = jnp.zeros((6, HD), jnp.float32)
            either(
                back_self(yy, xx),
                lambda yy=yy, xx=xx: back_stats(yy, xx).start(),
                lambda yy=yy, xx=xx: back_stats_here(yy, xx),
            )
            return_half(yy, xx, 0)
    for yy in order:
        for xx in range(2):
            return_half(yy, xx, 1)

    def merge(n):
        for j in range(4):
            for xx in range(2):
                landed(o_in.at[xx, j, halves[n]], ot_r.at[n, xx, j])
                if n == 0:
                    landed(st_in.at[xx, j], st_r.at[xx, j])
            one, two = st_in[0, j, halves[n]], st_in[1, j, halves[n]]
            peak = jnp.maximum(one[0:1], two[0:1])
            a0 = one[1:2] * jnp.exp2(one[0:1] - peak)
            a1 = two[1:2] * jnp.exp2(two[0:1] - peak)
            whole = a0 + a1
            merged = o_in[0, j, halves[n]].astype(jnp.float32) * (a0 / whole) + o_in[
                1, j, halves[n]
            ].astype(jnp.float32) * (a1 / whole)
            att[n, :, j * HD:(j + 1) * HD] = merged.T.astype(jnp.bfloat16)

    def to_sib(h, n):
        return remote(
            p_sib.at[h, n], sib_in.at[h, n], sb_s.at[h, n], sb_r.at[h, n], dev(y, z, x, 1 - c)
        )

    def to_cut(n):
        return remote(cut_out.at[n], cut_in.at[n], cu_s.at[n], cu_r.at[n], dev(y, z, x, c, 1 - xh))

    def project(h, n):
        cols = pl.ds(pl.multiple_of(n * CH, CH), CH)
        part = jnp.dot(att[h], w_vm[:, cols], preferred_element_type=jnp.float32)

        @pl.when(c == 0)
        def _():
            p_own[h, n] = part[:64]
            p_sib[h, n] = part[64:].astype(jnp.bfloat16)

        @pl.when(c == 1)
        def _():
            p_own[h, n] = part[64:]
            p_sib[h, n] = part[:64].astype(jnp.bfloat16)

        to_sib(h, n).start()

    def reduce_chip(n):
        to_sib(0, n).wait_recv()
        cut_out[n] = (p_own[0, n] + sib_in[0, n].astype(jnp.float32)).astype(jnp.bfloat16)
        to_cut(n).start()

    def first_turn(n, _):
        @pl.when(n < NCH)
        def _():
            project(0, n)

        @pl.when(n > 0)
        def _():
            reduce_chip(n - 1)

        return 0

    def second_turn(n, _):
        project(1, n)
        return 0

    def out_copy(n):
        return pltpu.make_async_copy(out_vm.at[n], o_ref.at[:, n * CH:(n + 1) * CH], out_s.at[n])

    merge(0)
    w_copy.wait()
    lax.fori_loop(0, NCH + 1, first_turn, 0)
    merge(1)
    lax.fori_loop(0, NCH, second_turn, 0)
    for n in range(NCH):
        to_sib(1, n).wait_recv()
        p_own[1, n] = p_own[1, n] + sib_in[1, n].astype(jnp.float32)
    for i in range(2):
        for n in range(2):
            either(kv_self(i, n), lambda i=i, n=n: kv_copy(i, n).wait_send(), None)
    for j in range(4):
        for xx in range(2):
            either(q_self(j, xx), lambda j=j, xx=xx: q_copy(j, xx).wait_send(), None)

    for yk in order:
        forwards(0, yk, lambda copy: copy.wait_send())
    for yk in order:
        share(0, yk).wait_send()

    def drain(s, _):
        for yk in order:
            forwards(s, yk, lambda copy: copy.wait_send())
            share(s, yk).wait_send()
        return 0

    lax.fori_loop(1, 8, drain, 0)
    for yy in range(4):
        for xx in range(2):
            either(
                back_self(yy, xx),
                lambda yy=yy, xx=xx: [
                    copy.wait_send()
                    for copy in (back_stats(yy, xx), back(yy, xx, 0), back(yy, xx, 1))
                ],
                None,
            )

    for n in range(NCH):
        to_cut(n).wait_recv()
        total = p_own[1, n] + cut_in[n].astype(jnp.float32)
        out_vm[n] = total.astype(jnp.bfloat16)
        out_copy(n).start()
    for n in range(NCH):
        out_copy(n).wait()
        to_sib(0, n).wait_send()
        to_sib(1, n).wait_send()
        to_cut(n).wait_send()


def per_device(queries, keys, values, doc_ids, out_weight):
    bf, f32 = jnp.bfloat16, jnp.float32
    vm, dma = pltpu.VMEM, pltpu.SemaphoreType.DMA
    scratch = [
        vm((T, 512), bf),
        vm((T, 256), bf),
        vm((T, 256), bf),
        pltpu.SMEM((128,), jnp.int32),
        vm((512, D), bf),
        vm((4, HD, T), bf),
        vm((2, 2, T, HD), bf),
        vm((2, NZ, NY, T, HD), bf),
        vm((NY, NX, HD, T), bf),
        vm((NY, 2 * HD, 2 * T), bf),
        vm((NY, 1, 2 * T), f32),
        vm((NY, 1, 2 * T), f32),
        vm((NY, HD, 2 * T), f32),
        vm((NY, NX, 2, HD, HD), bf),
        vm((NY, NX, 2, 8, HD), f32),
        vm((NX, 4, 2, HD, HD), bf),
        vm((NX, 4, 2, 8, HD), f32),
        vm((2, HD, 512), bf),
        vm((2, NCH, 64, CH), f32),
        vm((2, NCH, 64, CH), bf),
        vm((2, NCH, 64, CH), bf),
        vm((NCH, 64, CH), bf),
        vm((NCH, 64, CH), bf),
        vm((NCH, 64, CH), bf),
        dma((4,)),
        dma((NCH,)),
        dma,
        dma((2, 2)),
        dma((4, 2)),
        dma((8, 4)),
        dma((8, 4)),
        dma((8, 4)),
        dma((8, 4)),
        dma((4, 2)),
        dma((2, 4, 2)),
        dma((2, 2, 4)),
        dma((4, 2)),
        dma((2, 4)),
        dma((2, NCH)),
        dma((2, NCH)),
        dma((NCH,)),
        dma((NCH,)),
    ]
    return pl.pallas_call(
        kernel,
        out_shape=jax.ShapeDtypeStruct((64, D), bf),
        in_specs=[pl.BlockSpec(memory_space=pltpu.HBM)] * 5,
        out_specs=pl.BlockSpec(memory_space=pltpu.HBM),
        scratch_shapes=scratch,
        compiler_params=pltpu.CompilerParams(
            collective_id=0, has_side_effects=True, vmem_limit_bytes=64 * 2**20
        ),
    )(queries, keys, values, doc_ids, out_weight)


def solution(mesh):
    placed = (P("ctx", "head"), P("ctx", "head"), P("ctx", "head"), P(), P("head", None))
    return jax.shard_map(
        per_device, mesh=mesh, in_specs=placed, out_specs=P(("ctx", "head"), None), check_vma=False
    )
```

```python
import functools

import jax
import jax.numpy as jnp
import numpy as np
from jax import lax
from jax.experimental import pallas as pl
from jax.experimental.pallas import tpu as pltpu
from jax.sharding import PartitionSpec as P

MESH = pl.DeviceIdType.MESH
HD = 128
T = 256
NY, NZ, NX = 4, 8, 2
D = 5376
CH = 768
NCH = D // CH
QSCALE = float(168.0 ** (-0.5) * np.log2(np.e))
NEG = -1e30


def kernel(
    q_hbm, k_hbm, v_hbm, doc_hbm, w_ref, o_ref, q_ref, k_ref, v_ref, doc_ref,
    w_vm, qsrc, ksrc, kv, q_in, qt, m_s, l_s, acc, o_out, st_out, o_in, st_in,
    att, p_own, p_sib, sib_in, cut_out, cut_in, out_vm,
    in_s, out_s, w_sem, a_kv_s, a_q_s, r_sem, f_sem, h_s, h_r, q_r, ot_s, ot_r, st_s, st_r,
    sb_s, sb_r, cu_s, cu_r,
):
    ctx, head = lax.axis_index("ctx"), lax.axis_index("head")
    y, z, x = ctx // 16, (ctx // 2) % 8, ctx % 2
    xh, c = head // 2, head % 2

    def dev(yy, zz, xx, cc, hh=xh):
        return {"ctx": (yy * 8 + zz) * 2 + xx, "head": hh * 2 + cc}

    def remote(src, dst, s, r, to):
        return pltpu.make_async_remote_copy(
            src_ref=src, dst_ref=dst, send_sem=s, recv_sem=r, device_id=to, device_id_type=MESH
        )

    loads = [
        pltpu.make_async_copy(src, dst, in_s.at[i])
        for i, (src, dst) in enumerate(
            ((q_hbm, q_ref), (k_hbm, k_ref), (v_hbm, v_ref), (doc_hbm, doc_ref))
        )
    ]
    for load in loads:
        load.start()
    barrier = pltpu.get_barrier_semaphore()

    def greet(to):
        pl.semaphore_signal(barrier, inc=1, device_id=to, device_id_type=MESH)

    for i in range(1, 16):
        greet(dev((y + i // 4) % 4, z, (x + (i // 2) % 2) % 2, (c + i) % 2))
    up, down = (z + 1) % 8, (z + 7) % 8
    greet(dev(y, up, x, c))
    greet(dev(y, down, x, c))
    greet(dev(y, z, x, c, 1 - xh))

    w_copy = pltpu.make_async_copy(w_ref, w_vm, w_sem)
    w_copy.start()

    for load in loads:
        load.wait()
    for i in range(2):
        ksrc[0, i] = k_ref[:, i * HD:(i + 1) * HD]
        for t in range(2):
            part = v_ref[t * HD:(t + 1) * HD, i * HD:(i + 1) * HD]
            ksrc[1, i, t * HD:(t + 1) * HD, :] = part.astype(jnp.float32).T.astype(jnp.bfloat16)
    for j in range(4):
        part = q_ref[:, j * HD:(j + 1) * HD]
        qsrc[j] = part.astype(jnp.float32).T.astype(jnp.bfloat16)
    m_s[...] = jnp.full(m_s.shape, NEG, jnp.float32)
    l_s[...] = jnp.zeros(l_s.shape, jnp.float32)
    acc[...] = jnp.zeros(acc.shape, jnp.float32)

    pl.semaphore_wait(barrier, 18)

    def kv_copy(i, n):
        return remote(
            ksrc.at[n, i], kv.at[n, z, y], a_kv_s.at[n, i], r_sem.at[0, y], dev(2 * c + i, z, x, n)
        )

    def kv_self(i, n):
        return (2 * c + i == y) & (c == n)

    def q_copy(j, xx):
        return remote(
            qsrc.at[j], q_in.at[y, x], a_q_s.at[j, xx], q_r.at[y, x],
            dev(2 * c + j // 2, z, xx, j % 2),
        )

    def q_self(j, xx):
        return (2 * c + j // 2 == y) & (c == j % 2) & (xx == x)

    def either(cond, there, here):
        @pl.when(jnp.logical_not(cond))
        def _():
            there()

        if here is not None:

            @pl.when(cond)
            def _():
                here()

    for i in range(2):
        for n in range(2):
            either(
                kv_self(i, n),
                lambda i=i, n=n: kv_copy(i, n).start(),
                lambda i=i, n=n: pltpu.make_async_copy(
                    ksrc.at[n, i], kv.at[n, z, y], r_sem.at[0, y]
                ).start(),
            )
    def place(s):
        dist = (s + 1) // 2
        return (z + 8 + jnp.where(s % 2 == 1, -dist, dist)) % 8

    def pass_on(s, yk, to_slot, to_z):
        zz = place(s)
        return remote(
            kv.at[c, zz, yk], kv.at[c, zz, yk], f_sem.at[to_slot, yk], r_sem.at[to_slot, yk],
            dev(y, to_z, x, c),
        )

    def share(s, yk):
        zz = place(s)
        return remote(
            kv.at[c, zz, yk], kv.at[c, zz, yk], h_s.at[s, yk], h_r.at[s, yk], dev(y, z, x, 1 - c)
        )

    def landed(ref, sem):
        pltpu.make_async_copy(ref, ref, sem).wait()

    def forwards(s, yk, act):
        @pl.when(s == 0)
        def _():
            act(pass_on(s, yk, 1, up))
            act(pass_on(s, yk, 2, down))

        @pl.when((s > 0) & (s < 5))
        def _():
            act(pass_on(s, yk, s + 2, jnp.where(s % 2 == 1, up, down)))

        @pl.when((s == 5) & (c == 0))
        def _():
            act(pass_on(s, yk, 7, up))

        @pl.when((s == 6) & (c == 1))
        def _():
            act(pass_on(s, yk, 7, down))

    order = (3, 0, 1, 2)

    def arrive(s, yk):
        landed(kv.at[c, place(s), yk], r_sem.at[s, yk])
        forwards(s, yk, lambda copy: copy.start())
        share(s, yk).start()

    def chunk(n):
        return (y + n + (n == 2) * 1 - (n == 3) * 1) % 4

    def event(e, _):
        n = e % 4
        s, yk = 2 * (e // 4) + 1, (y + n + jnp.where(n == 2, 1, jnp.where(n == 3, -1, 0))) % 4
        arrive(s, yk)

        @pl.when(s < 7)
        def _():
            arrive(s + 1, yk)

        return 0

    def scores_of(yq, zz, yk, masked):
        kb = kv[0, zz, yk]
        scores = jnp.dot(
            jnp.concatenate([kb, kb], axis=1), qt[yq], preferred_element_type=jnp.float32
        )
        if masked:
            row = lax.broadcasted_iota(jnp.int32, (T, 1), 0)
            col = lax.broadcasted_iota(jnp.int32, (1, 2 * T), 1)
            kbase, qbase = (16 * yk + 2 * zz + x) * 2, (16 * yq + 2 * z) * 2
            kdoc = jnp.where(row < HD, doc_ref[kbase], doc_ref[kbase + 1])
            qdoc = jnp.where(
                col < HD, doc_ref[qbase],
                jnp.where(
                    col < 2 * HD, doc_ref[qbase + 1],
                    jnp.where(col < 3 * HD, doc_ref[qbase + 2], doc_ref[qbase + 3]),
                ),
            )
            allowed = (kdoc == qdoc) & (row + kbase * HD <= col + qbase * HD)
            scores = jnp.where(allowed, scores, NEG)
        return scores

    def soften(yq, scores):
        old = m_s[yq]
        new = jnp.maximum(old, jnp.max(scores, axis=0, keepdims=True))
        m_s[yq] = new
        return jnp.exp2(scores - new).astype(jnp.bfloat16), jnp.exp2(old - new)

    def add_values(yq, zz, yk, weights, shrink):
        vb = kv[1, zz, yk]
        vt = jnp.concatenate([vb[:HD], vb[HD:]], axis=1)
        vt = jnp.concatenate([vt, jnp.ones((16, T), jnp.bfloat16)], axis=0)
        added = jnp.dot(vt, weights, preferred_element_type=jnp.float32)
        l_s[yq] = l_s[yq] * shrink + added[HD:HD + 1]
        acc[yq] = acc[yq] * shrink + added[:HD]

    def attend(zz, pieces):
        scores = [scores_of(yq, zz, yk, masked) for yq, yk, masked in pieces]
        soft = [soften(piece[0], one) for piece, one in zip(pieces, scores)]
        for (yq, yk, _), (weights, shrink) in zip(pieces, soft):
            add_values(yq, zz, yk, weights, shrink)

    before = [(2, 0, False), (1, 0, False), (2, 1, False)]

    def compute(s):
        zz = place(s)
        for yk in order:
            landed(kv.at[1 - c, zz, yk], h_r.at[s, yk])

        @pl.when(zz > z)
        def _():
            attend(zz, before)

        @pl.when(zz < z)
        def _():
            attend(zz, before + [(0, 0, False), (2, 2, False), (1, 1, False), (3, 3, True)])

        @pl.when(zz == z)
        def _():
            attend(zz, before + [(0, 0, True), (2, 2, True), (1, 1, True), (3, 3, True)])

    def send_queries():
        for j in range(4):
            for xx in range(2):
                either(
                    q_self(j, xx),
                    lambda j=j, xx=xx: q_copy(j, xx).start(),
                    lambda j=j, xx=xx: pltpu.make_async_copy(
                        qsrc.at[j], q_in.at[y, x], q_r.at[y, x]
                    ).start(),
                )

    for n in range(4):
        arrive(0, chunk(n))
    send_queries()
    lax.fori_loop(0, 4, event, 0)
    for yy in range(4):
        for xx in range(2):
            landed(q_in.at[yy, xx], q_r.at[yy, xx])
            scaled = q_in[yy, xx].astype(jnp.float32) * QSCALE
            hi = scaled.astype(jnp.bfloat16)
            qt[yy, :HD, xx * T:(xx + 1) * T] = hi
            qt[yy, HD:, xx * T:(xx + 1) * T] = (scaled - hi.astype(jnp.float32)).astype(jnp.bfloat16)

    def seen(n):
        return 4 + n + jnp.where(n < 3, 2, jnp.where(n < 4, 3, jnp.where(n < 7, 4, 5)))

    def turn(n, _):
        lax.fori_loop(jnp.where(n < 1, 4, seen(n - 1)), seen(n), event, 0)
        compute(n)
        return 0

    lax.fori_loop(0, 8, turn, 0)

    halves = (1 - xh, xh)

    def back(yy, xx, n):
        j = 2 * (y % 2) + c
        return remote(
            o_out.at[yy, xx, halves[n]], o_in.at[x, j, halves[n]],
            ot_s.at[n, yy, xx], ot_r.at[n, x, j], dev(yy, z, xx, y // 2),
        )

    def back_stats(yy, xx):
        j = 2 * (y % 2) + c
        return remote(
            st_out.at[yy, xx], st_in.at[x, j], st_s.at[yy, xx], st_r.at[x, j],
            dev(yy, z, xx, y // 2),
        )

    def back_self(yy, xx):
        return (yy == y) & (xx == x) & (c == y // 2)

    def back_here(yy, xx, n):
        j = 2 * (y % 2) + c
        pltpu.make_async_copy(
            o_out.at[yy, xx, halves[n]], o_in.at[x, j, halves[n]], ot_r.at[n, x, j]
        ).start()

    def back_stats_here(yy, xx):
        j = 2 * (y % 2) + c
        pltpu.make_async_copy(st_out.at[yy, xx], st_in.at[x, j], st_r.at[x, j]).start()

    def return_half(yy, xx, n):
        either(
            back_self(yy, xx),
            lambda: back(yy, xx, n).start(),
            lambda: back_here(yy, xx, n),
        )

    for yy in map(chunk, (3, 1, 2, 0)):
        part = (acc[yy] * (1.0 / l_s[yy])).astype(jnp.bfloat16)
        for xx in range(2):
            for th in range(2):
                lanes = slice(xx * T + th * HD, xx * T + (th + 1) * HD)
                o_out[yy, xx, th] = part[:, lanes]
                st_out[yy, xx, th, 0:1] = m_s[yy][:, lanes]
                st_out[yy, xx, th, 1:2] = l_s[yy][:, lanes]
                st_out[yy, xx, th, 2:8] = jnp.zeros((6, HD), jnp.float32)
            either(
                back_self(yy, xx),
                lambda yy=yy, xx=xx: back_stats(yy, xx).start(),
                lambda yy=yy, xx=xx: back_stats_here(yy, xx),
            )
            return_half(yy, xx, 0)
    for yy in map(chunk, (3, 1, 2, 0)):
        for xx in range(2):
            return_half(yy, xx, 1)

    def merge(n):
        for j in range(4):
            for xx in range(2):
                landed(o_in.at[xx, j, halves[n]], ot_r.at[n, xx, j])
                if n == 0:
                    landed(st_in.at[xx, j], st_r.at[xx, j])
            one, two = st_in[0, j, halves[n]], st_in[1, j, halves[n]]
            peak = jnp.maximum(one[0:1], two[0:1])
            a0 = one[1:2] * jnp.exp2(one[0:1] - peak)
            a1 = two[1:2] * jnp.exp2(two[0:1] - peak)
            whole = a0 + a1
            merged = o_in[0, j, halves[n]].astype(jnp.float32) * (a0 / whole) + o_in[
                1, j, halves[n]
            ].astype(jnp.float32) * (a1 / whole)
            att[n, :, j * HD:(j + 1) * HD] = merged.T.astype(jnp.bfloat16)

    def to_sib(h, n):
        return remote(
            p_sib.at[h, n], sib_in.at[h, n], sb_s.at[h, n], sb_r.at[h, n], dev(y, z, x, 1 - c)
        )

    def to_cut(n):
        return remote(cut_out.at[n], cut_in.at[n], cu_s.at[n], cu_r.at[n], dev(y, z, x, c, 1 - xh))

    def project(h, n):
        cols = pl.ds(pl.multiple_of(n * CH, CH), CH)
        part = jnp.dot(att[h], w_vm[:, cols], preferred_element_type=jnp.float32)

        @pl.when(c == 0)
        def _():
            p_own[h, n] = part[:64]
            p_sib[h, n] = part[64:].astype(jnp.bfloat16)

        @pl.when(c == 1)
        def _():
            p_own[h, n] = part[64:]
            p_sib[h, n] = part[:64].astype(jnp.bfloat16)

        to_sib(h, n).start()

    def reduce_chip(n):
        to_sib(0, n).wait_recv()
        cut_out[n] = (p_own[0, n] + sib_in[0, n].astype(jnp.float32)).astype(jnp.bfloat16)
        to_cut(n).start()

    def first_turn(n, _):
        @pl.when(n < NCH)
        def _():
            project(0, n)

        @pl.when(n > 0)
        def _():
            reduce_chip(n - 1)

        return 0

    def second_turn(n, _):
        project(1, n)
        return 0

    def out_copy(n):
        return pltpu.make_async_copy(out_vm.at[n], o_ref.at[:, n * CH:(n + 1) * CH], out_s.at[n])

    merge(0)
    w_copy.wait()
    lax.fori_loop(0, NCH + 1, first_turn, 0)
    merge(1)
    lax.fori_loop(0, NCH, second_turn, 0)
    for n in range(NCH):
        to_sib(1, n).wait_recv()
        p_own[1, n] = p_own[1, n] + sib_in[1, n].astype(jnp.float32)
    for i in range(2):
        for n in range(2):
            either(kv_self(i, n), lambda i=i, n=n: kv_copy(i, n).wait_send(), None)
    for j in range(4):
        for xx in range(2):
            either(q_self(j, xx), lambda j=j, xx=xx: q_copy(j, xx).wait_send(), None)

    for yk in order:
        forwards(0, yk, lambda copy: copy.wait_send())
    for yk in order:
        share(0, yk).wait_send()

    def drain(s, _):
        for yk in order:
            forwards(s, yk, lambda copy: copy.wait_send())
            share(s, yk).wait_send()
        return 0

    lax.fori_loop(1, 8, drain, 0)
    for yy in range(4):
        for xx in range(2):
            either(
                back_self(yy, xx),
                lambda yy=yy, xx=xx: [
                    copy.wait_send()
                    for copy in (back_stats(yy, xx), back(yy, xx, 0), back(yy, xx, 1))
                ],
                None,
            )

    for n in range(NCH):
        to_cut(n).wait_recv()
        total = p_own[1, n] + cut_in[n].astype(jnp.float32)
        out_vm[n] = total.astype(jnp.bfloat16)
        out_copy(n).start()
    for n in range(NCH):
        out_copy(n).wait()
        to_sib(0, n).wait_send()
        to_sib(1, n).wait_send()
        to_cut(n).wait_send()


def per_device(queries, keys, values, doc_ids, out_weight):
    bf, f32 = jnp.bfloat16, jnp.float32
    vm, dma = pltpu.VMEM, pltpu.SemaphoreType.DMA
    scratch = [
        vm((T, 512), bf),
        vm((T, 256), bf),
        vm((T, 256), bf),
        pltpu.SMEM((128,), jnp.int32),
        vm((512, D), bf),
        vm((4, HD, T), bf),
        vm((2, 2, T, HD), bf),
        vm((2, NZ, NY, T, HD), bf),
        vm((NY, NX, HD, T), bf),
        vm((NY, 2 * HD, 2 * T), bf),
        vm((NY, 1, 2 * T), f32),
        vm((NY, 1, 2 * T), f32),
        vm((NY, HD, 2 * T), f32),
        vm((NY, NX, 2, HD, HD), bf),
        vm((NY, NX, 2, 8, HD), f32),
        vm((NX, 4, 2, HD, HD), bf),
        vm((NX, 4, 2, 8, HD), f32),
        vm((2, HD, 512), bf),
        vm((2, NCH, 64, CH), f32),
        vm((2, NCH, 64, CH), bf),
        vm((2, NCH, 64, CH), bf),
        vm((NCH, 64, CH), bf),
        vm((NCH, 64, CH), bf),
        vm((NCH, 64, CH), bf),
        dma((4,)),
        dma((NCH,)),
        dma,
        dma((2, 2)),
        dma((4, 2)),
        dma((8, 4)),
        dma((8, 4)),
        dma((8, 4)),
        dma((8, 4)),
        dma((4, 2)),
        dma((2, 4, 2)),
        dma((2, 2, 4)),
        dma((4, 2)),
        dma((2, 4)),
        dma((2, NCH)),
        dma((2, NCH)),
        dma((NCH,)),
        dma((NCH,)),
    ]
    return pl.pallas_call(
        kernel,
        out_shape=jax.ShapeDtypeStruct((64, D), bf),
        in_specs=[pl.BlockSpec(memory_space=pltpu.HBM)] * 5,
        out_specs=pl.BlockSpec(memory_space=pltpu.HBM),
        scratch_shapes=scratch,
        compiler_params=pltpu.CompilerParams(
            collective_id=0, has_side_effects=True, vmem_limit_bytes=64 * 2**20
        ),
    )(queries, keys, values, doc_ids, out_weight)


def solution(mesh):
    placed = (P("ctx", "head"), P("ctx", "head"), P("ctx", "head"), P(), P("head", None))
    return jax.shard_map(
        per_device, mesh=mesh, in_specs=placed, out_specs=P(("ctx", "head"), None), check_vma=False
    )
```

```python
import functools

import jax
import jax.numpy as jnp
import numpy as np
from jax import lax
from jax.experimental import pallas as pl
from jax.experimental.pallas import tpu as pltpu
from jax.sharding import PartitionSpec as P

MESH = pl.DeviceIdType.MESH
HD = 128
T = 256
NY, NZ, NX = 4, 8, 2
D = 5376
CH = 768
NCH = D // CH
QSCALE = float(168.0 ** (-0.5) * np.log2(np.e))
NEG = -1e30


def kernel(
    q_hbm, k_hbm, v_hbm, doc_hbm, w_ref, o_ref, q_ref, k_ref, v_ref, doc_ref,
    w_vm, qsrc, ksrc, kv, q_in, qt, m_s, l_s, acc, o_out, st_out, o_in, st_in,
    att, p_own, p_sib, sib_in, cut_out, cut_in, out_vm,
    in_s, out_s, w_sem, a_kv_s, a_q_s, r_sem, f_sem, h_s, h_r, q_r, ot_s, ot_r, st_s, st_r,
    sb_s, sb_r, cu_s, cu_r,
):
    ctx, head = lax.axis_index("ctx"), lax.axis_index("head")
    y, z, x = ctx // 16, (ctx // 2) % 8, ctx % 2
    xh, c = head // 2, head % 2

    def dev(yy, zz, xx, cc, hh=xh):
        return {"ctx": (yy * 8 + zz) * 2 + xx, "head": hh * 2 + cc}

    def remote(src, dst, s, r, to):
        return pltpu.make_async_remote_copy(
            src_ref=src, dst_ref=dst, send_sem=s, recv_sem=r, device_id=to, device_id_type=MESH
        )

    loads = [
        pltpu.make_async_copy(src, dst, in_s.at[i])
        for i, (src, dst) in enumerate(
            ((q_hbm, q_ref), (k_hbm, k_ref), (v_hbm, v_ref), (doc_hbm, doc_ref))
        )
    ]
    for load in loads:
        load.start()
    barrier = pltpu.get_barrier_semaphore()

    def greet(to):
        pl.semaphore_signal(barrier, inc=1, device_id=to, device_id_type=MESH)

    for i in range(1, 16):
        greet(dev((y + i // 4) % 4, z, (x + (i // 2) % 2) % 2, (c + i) % 2))
    up, down = (z + 1) % 8, (z + 7) % 8
    greet(dev(y, up, x, c))
    greet(dev(y, down, x, c))
    greet(dev(y, z, x, c, 1 - xh))

    w_copy = pltpu.make_async_copy(w_ref, w_vm, w_sem)
    w_copy.start()

    for load in loads:
        load.wait()
    for i in range(2):
        ksrc[0, i] = k_ref[:, i * HD:(i + 1) * HD]
        for t in range(2):
            part = v_ref[t * HD:(t + 1) * HD, i * HD:(i + 1) * HD]
            ksrc[1, i, t * HD:(t + 1) * HD, :] = part.astype(jnp.float32).T.astype(jnp.bfloat16)
    for j in range(4):
        part = q_ref[:, j * HD:(j + 1) * HD]
        qsrc[j] = part.astype(jnp.float32).T.astype(jnp.bfloat16)
    m_s[...] = jnp.full(m_s.shape, NEG, jnp.float32)
    l_s[...] = jnp.zeros(l_s.shape, jnp.float32)
    acc[...] = jnp.zeros(acc.shape, jnp.float32)

    pl.semaphore_wait(barrier, 18)

    def kv_copy(i, n):
        return remote(
            ksrc.at[n, i], kv.at[n, z, y], a_kv_s.at[n, i], r_sem.at[0, y], dev(2 * c + i, z, x, n)
        )

    def kv_self(i, n):
        return (2 * c + i == y) & (c == n)

    def q_copy(j, xx):
        return remote(
            qsrc.at[j], q_in.at[y, x], a_q_s.at[j, xx], q_r.at[y, x],
            dev(2 * c + j // 2, z, xx, j % 2),
        )

    def q_self(j, xx):
        return (2 * c + j // 2 == y) & (c == j % 2) & (xx == x)

    def either(cond, there, here):
        @pl.when(jnp.logical_not(cond))
        def _():
            there()

        if here is not None:

            @pl.when(cond)
            def _():
                here()

    for i in range(2):
        for n in range(2):
            either(
                kv_self(i, n),
                lambda i=i, n=n: kv_copy(i, n).start(),
                lambda i=i, n=n: pltpu.make_async_copy(
                    ksrc.at[n, i], kv.at[n, z, y], r_sem.at[0, y]
                ).start(),
            )
    def place(s):
        dist = (s + 1) // 2
        return (z + 8 + jnp.where(s % 2 == 1, -dist, dist)) % 8

    def pass_on(s, yk, to_slot, to_z):
        zz = place(s)
        return remote(
            kv.at[c, zz, yk], kv.at[c, zz, yk], f_sem.at[to_slot, yk], r_sem.at[to_slot, yk],
            dev(y, to_z, x, c),
        )

    def share(s, yk):
        zz = place(s)
        return remote(
            kv.at[c, zz, yk], kv.at[c, zz, yk], h_s.at[s, yk], h_r.at[s, yk], dev(y, z, x, 1 - c)
        )

    def used(s, yk):
        return (yk < 2) | (place(s) <= z)

    def landed(ref, sem):
        pltpu.make_async_copy(ref, ref, sem).wait()

    def forwards(s, yk, act):
        @pl.when(s == 0)
        def _():
            act(pass_on(s, yk, 1, up))
            act(pass_on(s, yk, 2, down))

        @pl.when((s > 0) & (s < 5))
        def _():
            act(pass_on(s, yk, s + 2, jnp.where(s % 2 == 1, up, down)))

        @pl.when((s == 5) & (c == 0))
        def _():
            act(pass_on(s, yk, 7, up))

        @pl.when((s == 6) & (c == 1))
        def _():
            act(pass_on(s, yk, 7, down))

    order = (3, 0, 1, 2)

    def arrive(s, yk):
        landed(kv.at[c, place(s), yk], r_sem.at[s, yk])
        forwards(s, yk, lambda copy: copy.start())

        @pl.when(used(s, yk))
        def _():
            share(s, yk).start()

    def chunk(n):
        return (y + n + (n == 2) * 1 - (n == 3) * 1) % 4

    def event(e, _):
        n = e % 4
        s, yk = 2 * (e // 4) + 1, (y + n + jnp.where(n == 2, 1, jnp.where(n == 3, -1, 0))) % 4
        arrive(s, yk)

        @pl.when(s < 7)
        def _():
            arrive(s + 1, yk)

        return 0

    def scores_of(yq, zz, yk, masked):
        kb = kv[0, zz, yk]
        scores = jnp.dot(
            jnp.concatenate([kb, kb], axis=1), qt[yq], preferred_element_type=jnp.float32
        )
        if masked:
            row = lax.broadcasted_iota(jnp.int32, (T, 1), 0)
            col = lax.broadcasted_iota(jnp.int32, (1, 2 * T), 1)
            kbase, qbase = (16 * yk + 2 * zz + x) * 2, (16 * yq + 2 * z) * 2
            kdoc = jnp.where(row < HD, doc_ref[kbase], doc_ref[kbase + 1])
            qdoc = jnp.where(
                col < HD, doc_ref[qbase],
                jnp.where(
                    col < 2 * HD, doc_ref[qbase + 1],
                    jnp.where(col < 3 * HD, doc_ref[qbase + 2], doc_ref[qbase + 3]),
                ),
            )
            allowed = (kdoc == qdoc) & (row + kbase * HD <= col + qbase * HD)
            scores = jnp.where(allowed, scores, NEG)
        return scores

    def soften(yq, scores):
        old = m_s[yq]
        new = jnp.maximum(old, jnp.max(scores, axis=0, keepdims=True))
        m_s[yq] = new
        return jnp.exp2(scores - new).astype(jnp.bfloat16), jnp.exp2(old - new)

    def add_values(yq, zz, yk, weights, shrink):
        vb = kv[1, zz, yk]
        vt = jnp.concatenate([vb[:HD], vb[HD:]], axis=1)
        vt = jnp.concatenate([vt, jnp.ones((16, T), jnp.bfloat16)], axis=0)
        added = jnp.dot(vt, weights, preferred_element_type=jnp.float32)
        l_s[yq] = l_s[yq] * shrink + added[HD:HD + 1]
        acc[yq] = acc[yq] * shrink + added[:HD]

    def attend(zz, pieces):
        scores = [scores_of(yq, zz, yk, masked) for yq, yk, masked in pieces]
        soft = [soften(piece[0], one) for piece, one in zip(pieces, scores)]
        for (yq, yk, _), (weights, shrink) in zip(pieces, soft):
            add_values(yq, zz, yk, weights, shrink)

    before = [(2, 0, False), (1, 0, False), (2, 1, False)]

    def compute(s):
        zz = place(s)
        for yk in order:

            @pl.when(used(s, yk))
            def _(yk=yk):
                landed(kv.at[1 - c, zz, yk], h_r.at[s, yk])

        @pl.when(zz > z)
        def _():
            attend(zz, before)

        @pl.when(zz < z)
        def _():
            attend(zz, before + [(0, 0, False), (2, 2, False), (1, 1, False), (3, 3, True)])

        @pl.when(zz == z)
        def _():
            attend(zz, before + [(0, 0, True), (2, 2, True), (1, 1, True), (3, 3, True)])

    def send_queries():
        for j in range(4):
            for xx in range(2):
                either(
                    q_self(j, xx),
                    lambda j=j, xx=xx: q_copy(j, xx).start(),
                    lambda j=j, xx=xx: pltpu.make_async_copy(
                        qsrc.at[j], q_in.at[y, x], q_r.at[y, x]
                    ).start(),
                )

    for n in range(4):
        arrive(0, chunk(n))
    send_queries()
    lax.fori_loop(0, 4, event, 0)
    for yy in range(4):
        for xx in range(2):
            landed(q_in.at[yy, xx], q_r.at[yy, xx])
            scaled = q_in[yy, xx].astype(jnp.float32) * QSCALE
            hi = scaled.astype(jnp.bfloat16)
            qt[yy, :HD, xx * T:(xx + 1) * T] = hi
            qt[yy, HD:, xx * T:(xx + 1) * T] = (scaled - hi.astype(jnp.float32)).astype(jnp.bfloat16)

    def seen(n):
        return 4 + n + jnp.where(n < 3, 2, jnp.where(n < 4, 3, jnp.where(n < 7, 4, 5)))

    def turn(n, _):
        lax.fori_loop(jnp.where(n < 1, 4, seen(n - 1)), seen(n), event, 0)
        compute(n)
        return 0

    lax.fori_loop(0, 8, turn, 0)

    halves = (1 - xh, xh)

    def back(yy, xx, n):
        j = 2 * (y % 2) + c
        return remote(
            o_out.at[yy, xx, halves[n]], o_in.at[x, j, halves[n]],
            ot_s.at[n, yy, xx], ot_r.at[n, x, j], dev(yy, z, xx, y // 2),
        )

    def back_stats(yy, xx):
        j = 2 * (y % 2) + c
        return remote(
            st_out.at[yy, xx], st_in.at[x, j], st_s.at[yy, xx], st_r.at[x, j],
            dev(yy, z, xx, y // 2),
        )

    def back_self(yy, xx):
        return (yy == y) & (xx == x) & (c == y // 2)

    def back_here(yy, xx, n):
        j = 2 * (y % 2) + c
        pltpu.make_async_copy(
            o_out.at[yy, xx, halves[n]], o_in.at[x, j, halves[n]], ot_r.at[n, x, j]
        ).start()

    def back_stats_here(yy, xx):
        j = 2 * (y % 2) + c
        pltpu.make_async_copy(st_out.at[yy, xx], st_in.at[x, j], st_r.at[x, j]).start()

    def return_half(yy, xx, n):
        either(
            back_self(yy, xx),
            lambda: back(yy, xx, n).start(),
            lambda: back_here(yy, xx, n),
        )

    for yy in map(chunk, (3, 1, 2, 0)):
        part = (acc[yy] * (1.0 / l_s[yy])).astype(jnp.bfloat16)
        for xx in range(2):
            for th in range(2):
                lanes = slice(xx * T + th * HD, xx * T + (th + 1) * HD)
                o_out[yy, xx, th] = part[:, lanes]
                st_out[yy, xx, th, 0:1] = m_s[yy][:, lanes]
                st_out[yy, xx, th, 1:2] = l_s[yy][:, lanes]
                st_out[yy, xx, th, 2:8] = jnp.zeros((6, HD), jnp.float32)
            either(
                back_self(yy, xx),
                lambda yy=yy, xx=xx: back_stats(yy, xx).start(),
                lambda yy=yy, xx=xx: back_stats_here(yy, xx),
            )
            return_half(yy, xx, 0)
    for yy in map(chunk, (3, 1, 2, 0)):
        for xx in range(2):
            return_half(yy, xx, 1)

    def merge(n):
        for j in range(4):
            for xx in range(2):
                landed(o_in.at[xx, j, halves[n]], ot_r.at[n, xx, j])
                if n == 0:
                    landed(st_in.at[xx, j], st_r.at[xx, j])
            one, two = st_in[0, j, halves[n]], st_in[1, j, halves[n]]
            peak = jnp.maximum(one[0:1], two[0:1])
            a0 = one[1:2] * jnp.exp2(one[0:1] - peak)
            a1 = two[1:2] * jnp.exp2(two[0:1] - peak)
            whole = a0 + a1
            merged = o_in[0, j, halves[n]].astype(jnp.float32) * (a0 / whole) + o_in[
                1, j, halves[n]
            ].astype(jnp.float32) * (a1 / whole)
            att[n, :, j * HD:(j + 1) * HD] = merged.T.astype(jnp.bfloat16)

    def to_sib(h, n):
        return remote(
            p_sib.at[h, n], sib_in.at[h, n], sb_s.at[h, n], sb_r.at[h, n], dev(y, z, x, 1 - c)
        )

    def to_cut(n):
        return remote(cut_out.at[n], cut_in.at[n], cu_s.at[n], cu_r.at[n], dev(y, z, x, c, 1 - xh))

    def project(h, n):
        cols = pl.ds(pl.multiple_of(n * CH, CH), CH)
        part = jnp.dot(att[h], w_vm[:, cols], preferred_element_type=jnp.float32)

        @pl.when(c == 0)
        def _():
            p_own[h, n] = part[:64]
            p_sib[h, n] = part[64:].astype(jnp.bfloat16)

        @pl.when(c == 1)
        def _():
            p_own[h, n] = part[64:]
            p_sib[h, n] = part[:64].astype(jnp.bfloat16)

        to_sib(h, n).start()

    def reduce_chip(n):
        to_sib(0, n).wait_recv()
        cut_out[n] = (p_own[0, n] + sib_in[0, n].astype(jnp.float32)).astype(jnp.bfloat16)
        to_cut(n).start()

    def first_turn(n, _):
        @pl.when(n < NCH)
        def _():
            project(0, n)

        @pl.when(n > 0)
        def _():
            reduce_chip(n - 1)

        return 0

    def second_turn(n, _):
        project(1, n)
        return 0

    def out_copy(n):
        return pltpu.make_async_copy(out_vm.at[n], o_ref.at[:, n * CH:(n + 1) * CH], out_s.at[n])

    merge(0)
    w_copy.wait()
    lax.fori_loop(0, NCH + 1, first_turn, 0)
    merge(1)
    lax.fori_loop(0, NCH, second_turn, 0)
    for n in range(NCH):
        to_sib(1, n).wait_recv()
        p_own[1, n] = p_own[1, n] + sib_in[1, n].astype(jnp.float32)
    for i in range(2):
        for n in range(2):
            either(kv_self(i, n), lambda i=i, n=n: kv_copy(i, n).wait_send(), None)
    for j in range(4):
        for xx in range(2):
            either(q_self(j, xx), lambda j=j, xx=xx: q_copy(j, xx).wait_send(), None)

    for yk in order:
        forwards(0, yk, lambda copy: copy.wait_send())
    for yk in order:
        share(0, yk).wait_send()

    def drain(s, _):
        for yk in order:
            forwards(s, yk, lambda copy: copy.wait_send())

            @pl.when(used(s, yk))
            def _(yk=yk):
                share(s, yk).wait_send()

        return 0

    lax.fori_loop(1, 8, drain, 0)
    for yy in range(4):
        for xx in range(2):
            either(
                back_self(yy, xx),
                lambda yy=yy, xx=xx: [
                    copy.wait_send()
                    for copy in (back_stats(yy, xx), back(yy, xx, 0), back(yy, xx, 1))
                ],
                None,
            )

    for n in range(NCH):
        to_cut(n).wait_recv()
        total = p_own[1, n] + cut_in[n].astype(jnp.float32)
        out_vm[n] = total.astype(jnp.bfloat16)
        out_copy(n).start()
    for n in range(NCH):
        out_copy(n).wait()
        to_sib(0, n).wait_send()
        to_sib(1, n).wait_send()
        to_cut(n).wait_send()


def per_device(queries, keys, values, doc_ids, out_weight):
    bf, f32 = jnp.bfloat16, jnp.float32
    vm, dma = pltpu.VMEM, pltpu.SemaphoreType.DMA
    scratch = [
        vm((T, 512), bf),
        vm((T, 256), bf),
        vm((T, 256), bf),
        pltpu.SMEM((128,), jnp.int32),
        vm((512, D), bf),
        vm((4, HD, T), bf),
        vm((2, 2, T, HD), bf),
        vm((2, NZ, NY, T, HD), bf),
        vm((NY, NX, HD, T), bf),
        vm((NY, 2 * HD, 2 * T), bf),
        vm((NY, 1, 2 * T), f32),
        vm((NY, 1, 2 * T), f32),
        vm((NY, HD, 2 * T), f32),
        vm((NY, NX, 2, HD, HD), bf),
        vm((NY, NX, 2, 8, HD), f32),
        vm((NX, 4, 2, HD, HD), bf),
        vm((NX, 4, 2, 8, HD), f32),
        vm((2, HD, 512), bf),
        vm((2, NCH, 64, CH), f32),
        vm((2, NCH, 64, CH), bf),
        vm((2, NCH, 64, CH), bf),
        vm((NCH, 64, CH), bf),
        vm((NCH, 64, CH), bf),
        vm((NCH, 64, CH), bf),
        dma((4,)),
        dma((NCH,)),
        dma,
        dma((2, 2)),
        dma((4, 2)),
        dma((8, 4)),
        dma((8, 4)),
        dma((8, 4)),
        dma((8, 4)),
        dma((4, 2)),
        dma((2, 4, 2)),
        dma((2, 2, 4)),
        dma((4, 2)),
        dma((2, 4)),
        dma((2, NCH)),
        dma((2, NCH)),
        dma((NCH,)),
        dma((NCH,)),
    ]
    return pl.pallas_call(
        kernel,
        out_shape=jax.ShapeDtypeStruct((64, D), bf),
        in_specs=[pl.BlockSpec(memory_space=pltpu.HBM)] * 5,
        out_specs=pl.BlockSpec(memory_space=pltpu.HBM),
        scratch_shapes=scratch,
        compiler_params=pltpu.CompilerParams(
            collective_id=0, has_side_effects=True, vmem_limit_bytes=64 * 2**20
        ),
    )(queries, keys, values, doc_ids, out_weight)


def solution(mesh):
    placed = (P("ctx", "head"), P("ctx", "head"), P("ctx", "head"), P(), P("head", None))
    return jax.shard_map(
        per_device, mesh=mesh, in_specs=placed, out_specs=P(("ctx", "head"), None), check_vma=False
    )
```
